32 devices in a mesh: seq: 16 (over z, x, core), chan: 2 (over y).
Axes of the slice: x: 2, y: 2, z: 4, core: 2. Of those that a mesh axis runs over, the one named last changes fastest.
Arguments:
- tokens: int32 [2048], P('seq'), may hold values from 0 to 3
- stem_weight: bfloat16 [5, 4, 768], replicated, may hold values from -2.5 to 2.5
- conv_weight: bfloat16 [5, 768, 768], P(None, None, 'chan'), may hold values from -0.09375 to 0.09375
- cotangent: bfloat16 [2048, 768], P('seq', 'chan'), may hold values from -6 to 6
Outputs:
- blended: bfloat16 [2048, 768], P('seq', 'chan')
- grad_conv: float32 [5, 768, 768], P(None, 'seq', 'chan')
- grad_stem: float32 [5, 4, 768], P(None, None, 'chan')
The draws below stay inside these ranges and needn't reach their ends.
All inputs are finite; a program needn't handle non-finite values.
Results may differ from the reference program's by a relative error of at most 0.012.
Values may be sent and summed in bfloat16 or wider, within the bound.
No kernel may reach another device: no remote copies, remote signals or barrier semaphores. Data moves between devices by JAX's collectives and lax.ppermute only.
A program may use at most 128 MiB of HBM per device.

```python
import math
import jax
import jax.numpy as jnp
from jax import lax

C = 768
KW = 5
LENGTH = 2048


def with_ends(entries, stream_key, smallest, largest):
    spot = [jax.random.randint(jax.random.fold_in(stream_key, axis), (), 0, length) for axis, length in enumerate(entries.shape)]
    widest = entries.shape.index(max(entries.shape))
    beside = spot[:widest] + [(spot[widest] + 1) % entries.shape[widest]] + spot[widest + 1:]
    return entries.at[tuple(spot)].set(smallest).at[tuple(beside)].set(largest)


def steps_of(rng, shape, shards, smallest, high):
    loudness, own = 1.0, jax.random.fold_in(rng, 6)
    for dim, parts in shards:
        steps = jnp.exp(jax.random.uniform(jax.random.fold_in(own, dim), (parts,), jnp.float32, smallest / len(shards), high / len(shards)))
        loudness = loudness * jnp.repeat(steps, shape[dim] // parts).reshape([-1 if axis == dim else 1 for axis in range(len(shape))])
    return loudness


def scatter_about(own_key, shape, scale, bound, shards=(), kind=jnp.bfloat16):
    values = scale * jax.random.normal(own_key, shape, jnp.float32)
    if shards:
        values = values * steps_of(own_key, shape, shards, -0.22, 0.18)
    return jnp.clip(values, -bound, bound).astype(kind)


def setup_inputs(seed: int = 0) -> dict:
    seeds = jax.random.split(jax.random.key(seed), 5)
    return {
        "tokens": with_ends(jax.random.randint(seeds[0], (LENGTH,), 0, 4), jax.random.fold_in(seeds[0], 1), 0, 3).astype(jnp.int32),
        "stem_weight": scatter_about(seeds[1], (KW, 4, C), KW ** -0.5, 2.5),
        "conv_weight": scatter_about(seeds[2], (KW, C, C), (KW * C) ** -0.5, 0.09375, ((2, 2),)),
        "cotangent": scatter_about(seeds[3], (LENGTH, C), 1.0, 6.0, ((0, 16), (1, 2))),
    }


def gelu_parts(values_in):
    coeff = math.sqrt(2.0 / math.pi)
    tanh_val = jnp.tanh(coeff * (values_in + 0.044715 * values_in ** 3))
    result = 0.5 * values_in * (1.0 + tanh_val)
    slopes = 0.5 * (1.0 + tanh_val) + 0.5 * values_in * (1.0 - tanh_val ** 2) * coeff * (1.0 + 3.0 * 0.044715 * values_in ** 2)
    return (result, slopes)

def strand(bases, out_grad, stem_weight, conv_weight):
    count = bases.shape[0]
    one_hot = (bases[:, None] == jnp.arange(4, dtype=jnp.int32)[None, :]).astype(jnp.bfloat16)
    padded_hot = jnp.pad(one_hot, ((2, 2), (0, 0)))
    stem_sum = jnp.zeros((count, stem_weight.shape[2]), jnp.float32)
    for k in range(KW):
        stem_sum = stem_sum + jnp.dot(padded_hot[k:k + count], stem_weight[k], preferred_element_type=jnp.float32)
    stem_act = stem_sum.astype(jnp.bfloat16)
    gelu_val, gelu_slope = gelu_parts(stem_act.astype(jnp.float32))
    act = gelu_val.astype(jnp.bfloat16)
    padded_act = jnp.pad(act, ((2, 2), (0, 0)))
    conv_sum = jnp.zeros((count, conv_weight.shape[2]), jnp.float32)
    for k in range(KW):
        conv_sum = conv_sum + jnp.dot(padded_act[k:k + count], conv_weight[k], preferred_element_type=jnp.float32)
    layer_out = stem_act.astype(jnp.float32) + conv_sum
    padded_grad = jnp.pad(out_grad, ((2, 2), (0, 0)))
    data_grad = jnp.zeros((count, conv_weight.shape[1]), jnp.float32)
    kernel_list = []
    for k in range(KW):
        data_grad = data_grad + jnp.dot(padded_grad[4 - k:4 - k + count], conv_weight[k].T, preferred_element_type=jnp.float32)
        kernel_list.append(jnp.dot(padded_act[k:k + count].T, out_grad, preferred_element_type=jnp.float32))
    stem_grad_in = data_grad * gelu_slope
    stem_list = []
    for k in range(KW):
        stem_list.append(jnp.dot(padded_hot[k:k + count].astype(jnp.float32).T, stem_grad_in, precision=lax.Precision.HIGHEST))
    return (layer_out, jnp.stack(kernel_list), jnp.stack(stem_list))

def reference(tokens, stem_weight, conv_weight, cotangent):
    half_cot = cotangent * 0.5
    out_fwd, kernel_fwd, stem_fwd = strand(tokens, half_cot, stem_weight, conv_weight)
    rc_bases = (3 - tokens[::-1]).astype(jnp.int32)
    out_rev, kernel_rev, stem_rev = strand(rc_bases, half_cot[::-1], stem_weight, conv_weight)
    blended = (0.5 * (out_fwd + out_rev[::-1])).astype(jnp.bfloat16)
    return (blended, kernel_fwd + kernel_rev, stem_fwd + stem_rev)
```

```python
import functools
import math

import jax
import jax.numpy as jnp
from jax import lax
from jax.experimental import pallas as pl
from jax.experimental.pallas import tpu as pltpu
from jax.sharding import PartitionSpec as P

VMEM = pl.BlockSpec(memory_space=pltpu.VMEM)
SMEM = pl.BlockSpec(memory_space=pltpu.SMEM)
LANES = 128


def swap(value, mask):
    count = lax.axis_size("seq")
    return lax.ppermute(value, "seq", [(i, i ^ mask) for i in range(count)])


def swap_chan(value):
    count = lax.axis_size("chan")
    return lax.ppermute(value, "chan", [(i, i ^ 1) for i in range(count)])


def swap_next_chip(value):
    count = lax.axis_size("seq")
    pairs = [(i, i + 1) for i in range(1, count - 1, 2)]
    return lax.ppermute(value, "seq", pairs + [(b, a) for a, b in pairs])


def round_up(value, step):
    return (value + step - 1) // step * step


def gelu_value(stem):
    tanh_val = jnp.tanh(math.sqrt(2.0 / math.pi) * (stem + 0.044715 * stem * stem * stem))
    return 0.5 * stem * (1.0 + tanh_val), tanh_val


def gelu_slope(stem, tanh_val):
    coeff = math.sqrt(2.0 / math.pi)
    return 0.5 * (1.0 + tanh_val) + 0.5 * stem * (1.0 - tanh_val * tanh_val) * coeff * (
        1.0 + 3.0 * 0.044715 * stem * stem
    )


def indicators(codes, taps, middle, reverse):
    width = codes.shape[1]
    rows = 32
    wide = jnp.broadcast_to(codes, (rows, width))
    row = lax.broadcasted_iota(jnp.int32, (rows, width), 0)
    if reverse:
        row = 4 * taps - 1 - row
    seen = jnp.zeros((rows, width), jnp.int32)
    for k in range(taps):
        moved = pltpu.roll(wide, (middle - k) % width, 1) if k != middle else wide
        seen = jnp.where((row >= 4 * k) & (row < 4 * k + 4), moved, seen)
    letter = jnp.where(row >= 0, row & 3, 8) + 1
    return (seen == letter).astype(jnp.float32).astype(jnp.bfloat16)


def dot(left, right, dims=((1,), (0,))):
    return lax.dot_general(left, right, (dims, ((), ())), preferred_element_type=jnp.float32)


def local_kernel(taps, chan_ref, codes_ref, stem_w_ref, conv_w_ref, cot_ref, blended_ref, keep_ref, send_ref, act_f, act_r, stem_own, dact_f, dact_r, grad):
    span = cot_ref.shape[0]
    half = cot_ref.shape[1]
    rows = act_f.shape[0]
    chan = chan_ref[0]
    codes = codes_ref[...]
    hot_f = indicators(codes, taps, 0, False)[:, :rows]
    hot_r = indicators(codes, taps, 0, True)[:, :rows]
    centre = lax.broadcasted_iota(jnp.int32, (32, LANES), 0)
    centre = ((centre >= 8) & (centre < 12)).astype(jnp.float32).astype(jnp.bfloat16)
    inside = dot(hot_f, centre, ((0,), (0,)))[:, :1]
    stem_w = stem_w_ref[...]
    slopes = []
    for hot, act in ((hot_f, act_f), (hot_r, act_r)):
        stem = dot(hot, stem_w, ((0,), (0,))).astype(jnp.bfloat16).astype(jnp.float32)
        value, tanh_val = gelu_value(stem)
        act[...] = (value * inside).astype(jnp.bfloat16).astype(jnp.float32)
        slopes.append(gelu_slope(stem, tanh_val) * inside)
        if hot is hot_f:
            stem_own[...] = stem
        else:
            stem_own[...] += stem
    cot = cot_ref[...]
    dact_f[...] = jnp.zeros_like(dact_f)
    dact_r[...] = jnp.zeros_like(dact_r)
    total = stem_own[pl.ds(2, span), pl.ds(pl.multiple_of(chan * half, LANES), half)]
    for k in range(taps):
        weight = conv_w_ref[k]
        both = (act_f[k : k + span] + act_r[taps - 1 - k : taps - 1 - k + span]).astype(jnp.bfloat16)
        total += dot(both, weight)
        part = dot(cot, weight, ((1,), (1,)))
        dact_f[k : k + span] += part
        dact_r[taps - 1 - k : taps - 1 - k + span] += part
    blended_ref[...] = (0.5 * total).astype(jnp.bfloat16)
    result = jnp.zeros(grad.shape, jnp.float32)
    for hot, dact, slope in ((hot_f, dact_f, slopes[0]), (hot_r, dact_r, slopes[1])):
        dstem = 0.5 * dact[...] * slope
        high = dstem.astype(jnp.bfloat16)
        low = (dstem - high.astype(jnp.float32)).astype(jnp.bfloat16)
        result += dot(hot, high) + dot(hot, low)
    grad[...] = result
    keep_ref[...] = grad[: keep_ref.shape[0], pl.ds(pl.multiple_of(chan * half, LANES), half)]
    send_ref[...] = grad[: keep_ref.shape[0], pl.ds(pl.multiple_of((1 - chan) * half, LANES), half)]


def local_part(chan, codes, stem_w, conv_w, cot):
    taps, full, half = conv_w.shape
    span = cot.shape[0]
    rows = round_up(span + taps - 1, 16)
    out_rows = round_up(4 * taps, 8)
    return pl.pallas_call(
        functools.partial(local_kernel, taps),
        out_shape=(
            jax.ShapeDtypeStruct((span, half), jnp.bfloat16),
            jax.ShapeDtypeStruct((out_rows, half), jnp.float32),
            jax.ShapeDtypeStruct((out_rows, half), jnp.float32),
        ),
        in_specs=[SMEM, VMEM, VMEM, VMEM, VMEM],
        out_specs=(VMEM, VMEM, VMEM),
        scratch_shapes=[pltpu.VMEM((rows, full), jnp.float32) for _ in range(5)] + [pltpu.VMEM((32, full), jnp.float32)],
        compiler_params=pltpu.CompilerParams(vmem_limit_bytes=48 * 2**20),
        cost_estimate=pl.CostEstimate(flops=6 * span * taps * full * half, bytes_accessed=2 * taps * full * half, transcendentals=2 * span * full),
        name="local_part",
    )(chan, codes, stem_w, conv_w, cot)


def acts_kernel(taps, place, seq_ref, codes_ref, stem_w_ref, out_ref, line):
    count, span = codes_ref.shape
    chans = stem_w_ref.shape[0]
    seq = seq_ref[0]
    line[...] = jnp.zeros_like(line)
    for b in range(count):
        line[:, LANES + b * span : LANES + (b + 1) * span] = codes_ref[pl.ds(place(seq ^ b), 1), :]
    codes = line[...]
    stem_w = stem_w_ref[...]
    acts = []
    for reverse in (False, True):
        hot = indicators(codes, taps, taps // 2, reverse)
        stem = dot(stem_w, hot).astype(jnp.bfloat16).astype(jnp.float32)
        value, _ = gelu_value(stem)
        acts.append(jnp.where(codes > 0, value, 0.0).astype(jnp.bfloat16).astype(jnp.float32))
    width = codes.shape[1]
    for k in range(taps):
        move = (taps // 2 - k) % width
        back = (k - taps // 2) % width
        ahead = pltpu.roll(acts[0], move, 1) if move else acts[0]
        behind = pltpu.roll(acts[1], back, 1) if back else acts[1]
        out_ref[k * chans : (k + 1) * chans, :] = (ahead + behind)[:, LANES : LANES + count * span].astype(jnp.bfloat16)


def acts_part(seq, codes, stem_w, taps, place):
    count, span = codes.shape
    chans = stem_w.shape[0]
    return pl.pallas_call(
        functools.partial(acts_kernel, taps, place),
        out_shape=jax.ShapeDtypeStruct((taps * chans, count * span), jnp.bfloat16),
        in_specs=[SMEM, VMEM, VMEM],
        out_specs=VMEM,
        scratch_shapes=[pltpu.VMEM((1, count * span + 2 * LANES), jnp.int32)],
        compiler_params=pltpu.CompilerParams(vmem_limit_bytes=48 * 2**20),
        cost_estimate=pl.CostEstimate(flops=128 * count * span * chans, bytes_accessed=2 * taps * chans * count * span, transcendentals=2 * count * span * chans),
        name="acts_part",
    )(seq, codes, stem_w)


def grad_kernel(taps, kept, blocks, seq_ref, acts_ref, *refs):
    g_refs, out_ref = refs[:-1], refs[-1]
    span = g_refs[0].shape[0] // blocks[0][1]
    chans = acts_ref.shape[0] // taps
    seq = seq_ref[0]
    total = jnp.zeros((acts_ref.shape[0], g_refs[0].shape[1]), jnp.float32)
    for ref, (masks, _) in zip(g_refs, blocks):
        for i, mask in enumerate(masks):
            at = pl.multiple_of((seq ^ mask) * span, LANES)
            total += dot(acts_ref[:, pl.ds(at, span)], ref[i * span : (i + 1) * span, :])
    for k in range(taps):
        out_ref[k] = 0.5 * total[k * chans : k * chans + kept]


def grad_part(seq, acts, arrays, masks, taps, kept):
    half = arrays[0].shape[1]
    blocks = [(m, len(m)) for m in masks]
    return pl.pallas_call(
        functools.partial(grad_kernel, taps, kept, blocks),
        out_shape=jax.ShapeDtypeStruct((taps, kept, half), jnp.float32),
        in_specs=[SMEM, VMEM] + [VMEM] * len(arrays),
        out_specs=VMEM,
        compiler_params=pltpu.CompilerParams(vmem_limit_bytes=48 * 2**20),
        cost_estimate=pl.CostEstimate(flops=2 * acts.shape[0] * acts.shape[1] * half, bytes_accessed=2 * acts.size, transcendentals=0),
        name="grad_part",
    )(seq, acts, *arrays)


def on_device(tokens, stem_weight, conv_weight, cotangent):
    count = lax.axis_size("seq")
    seq = lax.axis_index("seq")
    chan = lax.axis_index("chan")
    span = tokens.shape[0]
    taps, full, half = conv_weight.shape
    edge = taps - 1
    far = range(4, count, 4)
    seq_arg = seq.astype(jnp.int32).reshape(1)
    chan_arg = chan.astype(jnp.int32).reshape(1)

    codes = tokens + 1
    mate = swap(codes, 1)
    other = swap_next_chip(codes)
    even = seq % 2 == 0
    before = jnp.where(even, other, mate)[span - edge :]
    after = jnp.where(even, mate, other)[:edge]
    ext = jnp.concatenate([before, codes, after, jnp.zeros(round_up(span + 2 * edge, LANES) - span - 2 * edge, jnp.int32)])

    far_cot = [cotangent] + [swap(cotangent, m) for m in far]
    far_codes = [codes] + [swap(codes, m) for m in far]
    table = jnp.stack(far_codes)
    table = jnp.concatenate([table, swap(table, 2)])
    table = jnp.concatenate([table, swap(table, 1)])
    quarter = count // 4

    def place(m):
        return (m & 1) * (2 * quarter) + ((m >> 1) & 1) * quarter + (m >> 2)

    flat_w = stem_weight.reshape(4 * taps, full)
    flat_w = jnp.pad(flat_w, ((0, 32 - 4 * taps), (0, 0)))
    blended, keep, send = local_part(chan_arg, ext[None], flat_w, conv_weight, cotangent)

    own = full // count
    own_w = lax.dynamic_slice_in_dim(flat_w, seq * own, own, 1).T
    own_w = jnp.pad(own_w, ((0, round_up(own, 16) - own), (0, 0)))
    acts = acts_part(seq_arg, table, own_w, taps, place)

    stem_grad = keep + swap_chan(send)
    stem_grad = sum([swap(stem_grad, m) for m in far], stem_grad)
    stem_grad = stem_grad + swap(stem_grad, 2)
    stem_grad = stem_grad + swap(stem_grad, 1)

    near = [swap(c, 2) for c in far_cot]
    chips = jnp.concatenate(far_cot + near)
    mates = swap(chips, 1)
    masks = [4 * z + 2 * x for x in range(2) for z in range(quarter)]
    grad_conv = grad_part(seq_arg, acts, [chips, mates], [masks, [m + 1 for m in masks]], taps, own)
    return blended, grad_conv, stem_grad[: 4 * taps].reshape(taps, 4, half)


def solution(mesh):
    return jax.shard_map(
        on_device,
        mesh=mesh,
        in_specs=(P("seq"), P(), P(None, None, "chan"), P("seq", "chan")),
        out_specs=(P("seq", "chan"), P(None, "seq", "chan"), P(None, None, "chan")),
        check_vma=False,
    )
```

```python
import functools
import math

import jax
import jax.numpy as jnp
from jax import lax
from jax.experimental import pallas as pl
from jax.experimental.pallas import tpu as pltpu
from jax.sharding import PartitionSpec as P

VMEM = pl.BlockSpec(memory_space=pltpu.VMEM)
LANES = 128
LIMIT = 24 * 2**20
CHEAP = pl.CostEstimate(flops=0, bytes_accessed=0, transcendentals=0)


def swap(value, mask):
    count = lax.axis_size("seq")
    return lax.ppermute(value, "seq", [(i, i ^ mask) for i in range(count)])


def swap_chan(value):
    count = lax.axis_size("chan")
    return lax.ppermute(value, "chan", [(i, i ^ 1) for i in range(count)])


def swap_next_chip(value):
    count = lax.axis_size("seq")
    pairs = [(i, i + 1) for i in range(1, count - 1, 2)]
    return lax.ppermute(value, "seq", pairs + [(b, a) for a, b in pairs])


def round_up(value, step):
    return (value + step - 1) // step * step


def gelu_value(stem):
    tanh_val = jnp.tanh(math.sqrt(2.0 / math.pi) * (stem + 0.044715 * stem * stem * stem))
    return 0.5 * stem * (1.0 + tanh_val), tanh_val


def gelu_slope(stem, tanh_val):
    coeff = math.sqrt(2.0 / math.pi)
    return 0.5 * (1.0 + tanh_val) + 0.5 * stem * (1.0 - tanh_val * tanh_val) * coeff * (
        1.0 + 3.0 * 0.044715 * stem * stem
    )


def indicators(bases, taps, shift, width, reverse):
    rows = 32
    size = bases.shape[1]
    wide = jnp.broadcast_to(bases, (rows, size))
    row = lax.broadcasted_iota(jnp.int32, (rows, width), 0)
    if reverse:
        row = 4 * taps - 1 - row
    seen = jnp.full((rows, width), -1, jnp.int32)
    for k in range(taps):
        move = (-shift - k) % size
        moved = (pltpu.roll(wide, move, 1) if move else wide)[:, :width]
        seen = jnp.where((row >= 4 * k) & (row < 4 * k + 4), moved, seen)
    return (seen == (row & 3)).astype(jnp.float32).astype(jnp.bfloat16)


def dot(left, right, dims=((1,), (0,))):
    return lax.dot_general(left, right, (dims, ((), ())), preferred_element_type=jnp.float32)


def flat_kernel(stem_w_hbm, out_ref, stem_w_ref, sem):
    copy = pltpu.make_async_copy(stem_w_hbm, stem_w_ref, sem)
    copy.start()
    out_ref[...] = jnp.zeros_like(out_ref)
    copy.wait()
    for k in range(stem_w_ref.shape[0]):
        out_ref[4 * k : 4 * k + 4, :] = stem_w_ref[k].astype(jnp.float32)


def flat_part(stem_w):
    return pl.pallas_call(
        flat_kernel,
        out_shape=jax.ShapeDtypeStruct((32, stem_w.shape[2]), jnp.float32),
        in_specs=[pl.BlockSpec(memory_space=pl.ANY)],
        out_specs=VMEM,
        scratch_shapes=[pltpu.VMEM(stem_w.shape, stem_w.dtype), pltpu.SemaphoreType.DMA(())],
        cost_estimate=pl.CostEstimate(flops=6 * 10**9, bytes_accessed=0, transcendentals=0),
        name="flat_part",
    )(stem_w)


def line_of(own_ref, mate_ref, other_ref, line):
    span = own_ref.shape[1]
    seq = lax.axis_index("seq")
    even = lax.rem(seq, 2) == 0
    mate, other = mate_ref[...], other_ref[...]
    line[:, :span] = jnp.where(even, other, mate)
    line[:, span : 2 * span] = own_ref[...]
    line[:, 2 * span :] = jnp.where(even, mate, other)
    at = lax.broadcasted_iota(jnp.int32, line.shape, 1) + (seq - 1) * span
    return jnp.where((at >= 0) & (at < span * lax.axis_size("seq")), line[...], -1)


def centre_rows(taps):
    row = lax.broadcasted_iota(jnp.int32, (32, LANES), 0)
    reach = taps // 2
    return ((row >= 4 * reach) & (row < 4 * reach + 4)).astype(jnp.float32).astype(jnp.bfloat16)


def own_half(ref, rows, half, chan):
    return ref[rows, pl.ds(pl.multiple_of(chan * half, LANES), half)]


def back_kernel(cot_ref, conv_w, dact_f, dact_r):
    taps = conv_w.shape[0]
    span = cot_ref.shape[0]
    dact_f[...] = jnp.zeros_like(dact_f)
    dact_r[...] = jnp.zeros_like(dact_r)
    cot = cot_ref[...]
    for k in range(taps):
        part = dot(cot, conv_w[k], ((1,), (1,)))
        dact_f[k : k + span] += part
        dact_r[taps - 1 - k : taps - 1 - k + span] += part


def back_part(cot, conv_w):
    taps, full, _ = conv_w.shape
    rows = round_up(cot.shape[0] + taps - 1, 16)
    return pl.pallas_call(
        back_kernel,
        out_shape=tuple(jax.ShapeDtypeStruct((rows, full), jnp.float32) for _ in range(2)),
        in_specs=[VMEM] * 2,
        out_specs=(VMEM, VMEM),
        compiler_params=pltpu.CompilerParams(vmem_limit_bytes=LIMIT),
        cost_estimate=pl.CostEstimate(flops=14 * 10**8, bytes_accessed=0, transcendentals=0),
        name="back_part",
    )(cot, conv_w)


def stem_kernel(taps, dact_f, dact_r, own_ref, mate_ref, other_ref, flat, keep_ref, send_ref, line, grad):
    rows, full = dact_f.shape
    half = keep_ref.shape[1]
    span = own_ref.shape[1]
    seq, chan = lax.axis_index("seq"), lax.axis_index("chan")
    bases = line_of(own_ref, mate_ref, other_ref, line)
    stem_w = flat[...].astype(jnp.bfloat16)
    result = jnp.zeros(grad.shape, jnp.float32)
    for strand, dact in enumerate((dact_f, dact_r)):
        hot = indicators(bases, taps, span - 2 * (taps // 2), rows, strand == 1)
        if strand == 0:
            inside = dot(hot, centre_rows(taps), ((0,), (0,)))[:, :1]
        stem = dot(hot, stem_w, ((0,), (0,))).astype(jnp.bfloat16).astype(jnp.float32)
        _, tanh_val = gelu_value(stem)
        dstem = 0.5 * dact[...] * gelu_slope(stem, tanh_val) * inside
        high = dstem.astype(jnp.bfloat16)
        low = (dstem - high.astype(jnp.float32)).astype(jnp.bfloat16)
        result += dot(hot, high) + dot(hot, low)
    grad[...] = result
    top = send_ref.shape[0]
    keep_ref[:top, :] = own_half(grad, slice(0, top), half, chan)
    send_ref[...] = own_half(grad, slice(0, top), half, 1 - chan)
    per_row = half // span
    shape = (keep_ref.shape[0] - top, half)
    place = lax.broadcasted_iota(jnp.int32, shape, 0) * per_row + lax.broadcasted_iota(jnp.int32, shape, 1) // span
    table = jnp.zeros(shape, jnp.float32)
    for ref, block in ((own_ref, seq), (mate_ref, seq ^ 1)):
        row = jnp.broadcast_to(jnp.concatenate([ref[...].astype(jnp.float32)] * per_row, axis=1), shape)
        table = jnp.where(place == block, row, table)
    keep_ref[top:, :] = table


def stem_part(dacts, own, mate, other, flat, taps, half):
    full = flat.shape[1]
    span = own.shape[1]
    blocks = lax.axis_size("seq")
    per_row = half // span
    top = round_up(4 * taps, 8)
    rows = top + round_up((blocks + per_row - 1) // per_row, 8)
    return pl.pallas_call(
        functools.partial(stem_kernel, taps),
        out_shape=tuple(jax.ShapeDtypeStruct((r, half), jnp.float32) for r in (rows, top)),
        in_specs=[VMEM] * 6,
        out_specs=(VMEM, VMEM),
        scratch_shapes=[pltpu.VMEM((1, 3 * span), jnp.int32), pltpu.VMEM((32, full), jnp.float32)],
        compiler_params=pltpu.CompilerParams(vmem_limit_bytes=LIMIT),
        cost_estimate=CHEAP,
        name="stem_part",
    )(*dacts, own, mate, other, flat)


def blend_kernel(own_ref, mate_ref, other_ref, flat, conv_w, blended_ref, line, act_f, act_r, stem_own):
    taps = conv_w.shape[0]
    span, half = blended_ref.shape
    rows = act_f.shape[0]
    reach = taps // 2
    chan = lax.axis_index("chan")
    bases = line_of(own_ref, mate_ref, other_ref, line)
    stem_w = flat[...].astype(jnp.bfloat16)
    for strand, act in enumerate((act_f, act_r)):
        hot = indicators(bases, taps, span - 2 * reach, rows, strand == 1)
        if strand == 0:
            inside = dot(hot, centre_rows(taps), ((0,), (0,)))[:, :1]
        stem = dot(hot, stem_w, ((0,), (0,))).astype(jnp.bfloat16).astype(jnp.float32)
        value, _ = gelu_value(stem)
        act[...] = (value * inside).astype(jnp.bfloat16).astype(jnp.float32)
        if strand == 0:
            stem_own[...] = stem
        else:
            stem_own[...] += stem
    total = own_half(stem_own, pl.ds(reach, span), half, chan)
    for k in range(taps):
        back = taps - 1 - k
        both = (act_f[k : k + span] + act_r[back : back + span]).astype(jnp.bfloat16)
        total += dot(both, conv_w[k])
    blended_ref[...] = (0.5 * total).astype(jnp.bfloat16)


def blend_part(own, mate, other, flat, conv_w):
    taps, full, half = conv_w.shape
    span = own.shape[1]
    rows = round_up(span + taps - 1, 16)
    return pl.pallas_call(
        blend_kernel,
        out_shape=jax.ShapeDtypeStruct((span, half), jnp.bfloat16),
        in_specs=[VMEM] * 5,
        out_specs=VMEM,
        scratch_shapes=[pltpu.VMEM((1, 3 * span), jnp.int32)] + [pltpu.VMEM((rows, full), jnp.float32) for _ in range(3)],
        compiler_params=pltpu.CompilerParams(vmem_limit_bytes=LIMIT),
        cost_estimate=pl.CostEstimate(flops=2 * 10**9, bytes_accessed=0, transcendentals=0),
        name="blend_part",
    )(own, mate, other, flat, conv_w)


def grad_kernel(taps, kept, chans, masks, flat, table_ref, *refs):
    cots, out_ref, line, acts = refs[: len(masks)], *refs[len(masks) :]
    count = sum(map(len, masks))
    half = table_ref.shape[1]
    span = cots[0].shape[0] // len(masks[0])
    seq = lax.axis_index("seq")
    per_row = half // span
    top = round_up(4 * taps, 8)
    line[...] = jnp.full(line.shape, -1, jnp.int32)
    for b in range(count):
        row, lane = top + b // per_row, b % per_row * span
        line[:, LANES + b * span : LANES + (b + 1) * span] = table_ref[row : row + 1, lane : lane + span].astype(jnp.int32)
    bases = line[...]
    width = bases.shape[1]
    full = flat.shape[1]
    own_w = pltpu.roll(flat[...], lax.rem(full - seq * (full // count), full), 1)[:, :chans].astype(jnp.bfloat16)
    values = []
    reach = taps // 2
    for reverse in (False, True):
        hot = indicators(bases, taps, -reach, width, reverse)
        stem = dot(own_w, hot, ((0,), (0,))).astype(jnp.bfloat16).astype(jnp.float32)
        value, _ = gelu_value(stem)
        values.append(jnp.where(bases >= 0, value, 0.0).astype(jnp.bfloat16).astype(jnp.float32))
    order = [m for own in masks for m in own]
    for k in range(taps):
        move = (reach - k) % width
        back = (k - reach) % width
        ahead = pltpu.roll(values[0], move, 1) if move else values[0]
        behind = pltpu.roll(values[1], back, 1) if back else values[1]
        both = (ahead + behind).astype(jnp.bfloat16)
        for b in range(count):
            mask = seq ^ b
            slot = (mask & 3) * (count // 4) + lax.rem(count // 4 - (mask >> 2), count // 4)
            acts[k * chans : (k + 1) * chans, pl.ds(pl.multiple_of(slot * span, LANES), span)] = both[:, LANES + b * span : LANES + (b + 1) * span]
    total = jnp.zeros((taps * chans, half), jnp.float32)
    at = 0
    for ref in cots:
        total += dot(acts[:, at : at + ref.shape[0]], ref[...])
        at += ref.shape[0]
    for k in range(taps):
        out_ref[k] = 0.5 * total[k * chans : k * chans + kept]


def grad_part(flat, table, arrays, masks, span, taps):
    full = flat.shape[1]
    half = arrays[0].shape[1]
    count = sum(map(len, masks))
    kept = full // count
    chans = round_up(kept, 16)
    return pl.pallas_call(
        functools.partial(grad_kernel, taps, kept, chans, masks),
        out_shape=jax.ShapeDtypeStruct((taps, kept, half), jnp.float32),
        in_specs=[VMEM] * (2 + len(arrays)),
        out_specs=VMEM,
        scratch_shapes=[
            pltpu.VMEM((1, count * span + 2 * LANES), jnp.int32),
            pltpu.VMEM((taps * chans, count * span), jnp.bfloat16),
        ],
        compiler_params=pltpu.CompilerParams(vmem_limit_bytes=LIMIT),
        cost_estimate=pl.CostEstimate(flops=2 * 10**9, bytes_accessed=0, transcendentals=0),
        name="grad_part",
    )(flat, table, *arrays)


def after(value, *others):
    return lax.optimization_barrier((value, *others))[0]


def on_device(tokens, stem_weight, conv_weight, cotangent):
    count = lax.axis_size("seq")
    span = tokens.shape[0]
    taps, full, half = conv_weight.shape
    far = range(count - 4, 0, -4)

    bases = tokens.reshape(1, span)
    flat = flat_part(stem_weight)
    mate = swap(after(bases, flat), 1)
    cot = after(cotangent, flat)
    far_cot = [swap(cot, m) for m in far]
    other = swap_next_chip(bases)
    dacts = back_part(cot, conv_weight)
    keep, send = stem_part(dacts, bases, mate, other, flat, taps, half)
    got = swap_chan(send)
    total = jnp.concatenate([keep[: got.shape[0]] + got, keep[got.shape[0] :]])
    total, *far_cot = lax.optimization_barrier((total, *far_cot))
    here = jnp.concatenate([cotangent, *far_cot])
    there = swap(here, 2)
    here_mate = swap(here, 1)
    blended = blend_part(bases, mate, other, flat, conv_weight)
    for bit in range(2, (count - 1).bit_length()):
        total = total + swap(total, 1 << bit)
    total, here_mate, there, blended = lax.optimization_barrier((total, here_mate, there, blended))
    there_mate = swap(there, 1)
    total = total + swap(total, 2)
    total, there_mate = lax.optimization_barrier((total, there_mate))
    masks = [0, *far]
    masks = [[m + i for m in masks] for i in range(4)]
    grad_conv = grad_part(flat, total, [here, here_mate, there, there_mate], masks, span, taps)
    total = total[: 4 * taps] + swap(total[: 4 * taps], 1)
    return blended, grad_conv, total.reshape(taps, 4, half)


def solution(mesh):
    return jax.shard_map(
        on_device,
        mesh=mesh,
        in_specs=(P("seq"), P(), P(None, None, "chan"), P("seq", "chan")),
        out_specs=(P("seq", "chan"), P(None, "seq", "chan"), P(None, None, "chan")),
        check_vma=False,
    )
```

```python
import functools
import math

import jax
import jax.numpy as jnp
from jax import lax
from jax.experimental import pallas as pl
from jax.experimental.pallas import tpu as pltpu
from jax.sharding import PartitionSpec as P

VMEM = pl.BlockSpec(memory_space=pltpu.VMEM)
LANES = 128
LIMIT = 24 * 2**20
CHEAP = pl.CostEstimate(flops=0, bytes_accessed=0, transcendentals=0)


def swap(value, mask):
    count = lax.axis_size("seq")
    return lax.ppermute(value, "seq", [(i, i ^ mask) for i in range(count)])


def swap_chan(value):
    count = lax.axis_size("chan")
    return lax.ppermute(value, "chan", [(i, i ^ 1) for i in range(count)])


def swap_next_chip(value):
    count = lax.axis_size("seq")
    pairs = [(i, i + 1) for i in range(1, count - 1, 2)]
    return lax.ppermute(value, "seq", pairs + [(b, a) for a, b in pairs])


def round_up(value, step):
    return (value + step - 1) // step * step


def gelu_value(stem):
    tanh_val = jnp.tanh(math.sqrt(2.0 / math.pi) * (stem + 0.044715 * stem * stem * stem))
    return 0.5 * stem * (1.0 + tanh_val), tanh_val


def gelu_slope(stem, tanh_val):
    coeff = math.sqrt(2.0 / math.pi)
    return 0.5 * (1.0 + tanh_val) + 0.5 * stem * (1.0 - tanh_val * tanh_val) * coeff * (
        1.0 + 3.0 * 0.044715 * stem * stem
    )


def indicators(bases, taps, shift, width, reverse):
    rows = 32
    size = bases.shape[1]
    wide = jnp.broadcast_to(bases, (rows, size))
    row = lax.broadcasted_iota(jnp.int32, (rows, width), 0)
    if reverse:
        row = 4 * taps - 1 - row
    seen = jnp.full((rows, width), -1, jnp.int32)
    for k in range(taps):
        move = (-shift - k) % size
        moved = (pltpu.roll(wide, move, 1) if move else wide)[:, :width]
        seen = jnp.where((row >= 4 * k) & (row < 4 * k + 4), moved, seen)
    return (seen == (row & 3)).astype(jnp.float32).astype(jnp.bfloat16)


def dot(left, right, dims=((1,), (0,))):
    return lax.dot_general(left, right, (dims, ((), ())), preferred_element_type=jnp.float32)


def flat_kernel(stem_w_hbm, out_ref, stem_w_ref, sem):
    copy = pltpu.make_async_copy(stem_w_hbm, stem_w_ref, sem)
    copy.start()
    out_ref[...] = jnp.zeros_like(out_ref)
    copy.wait()
    for k in range(stem_w_ref.shape[0]):
        out_ref[4 * k : 4 * k + 4, :] = stem_w_ref[k].astype(jnp.float32)


def flat_part(stem_w):
    return pl.pallas_call(
        flat_kernel,
        out_shape=jax.ShapeDtypeStruct((32, stem_w.shape[2]), jnp.float32),
        in_specs=[pl.BlockSpec(memory_space=pl.ANY)],
        out_specs=VMEM,
        scratch_shapes=[pltpu.VMEM(stem_w.shape, stem_w.dtype), pltpu.SemaphoreType.DMA(())],
        cost_estimate=pl.CostEstimate(flops=6 * 10**9, bytes_accessed=0, transcendentals=0),
        name="flat_part",
    )(stem_w)


def line_of(own_ref, mate_ref, other_ref, line):
    span = own_ref.shape[1]
    seq = lax.axis_index("seq")
    even = lax.rem(seq, 2) == 0
    mate, other = mate_ref[...], other_ref[...]
    line[:, :span] = jnp.where(even, other, mate)
    line[:, span : 2 * span] = own_ref[...]
    line[:, 2 * span :] = jnp.where(even, mate, other)
    at = lax.broadcasted_iota(jnp.int32, line.shape, 1) + (seq - 1) * span
    return jnp.where((at >= 0) & (at < span * lax.axis_size("seq")), line[...], -1)


def centre_rows(taps):
    row = lax.broadcasted_iota(jnp.int32, (32, LANES), 0)
    reach = taps // 2
    return ((row >= 4 * reach) & (row < 4 * reach + 4)).astype(jnp.float32).astype(jnp.bfloat16)


def own_half(ref, rows, half, chan):
    return ref[rows, pl.ds(pl.multiple_of(chan * half, LANES), half)]


def back_kernel(cot_ref, conv_w, dact_f, dact_r):
    taps = conv_w.shape[0]
    span = cot_ref.shape[0]
    dact_f[...] = jnp.zeros_like(dact_f)
    dact_r[...] = jnp.zeros_like(dact_r)
    cot = cot_ref[...]
    for k in range(taps):
        part = dot(cot, conv_w[k], ((1,), (1,)))
        dact_f[k : k + span] += part
        dact_r[taps - 1 - k : taps - 1 - k + span] += part


def back_part(cot, conv_w):
    taps, full, _ = conv_w.shape
    rows = round_up(cot.shape[0] + taps - 1, 16)
    return pl.pallas_call(
        back_kernel,
        out_shape=tuple(jax.ShapeDtypeStruct((rows, full), jnp.float32) for _ in range(2)),
        in_specs=[VMEM] * 2,
        out_specs=(VMEM, VMEM),
        compiler_params=pltpu.CompilerParams(vmem_limit_bytes=LIMIT),
        cost_estimate=pl.CostEstimate(flops=14 * 10**8, bytes_accessed=0, transcendentals=0),
        name="back_part",
    )(cot, conv_w)


def stem_kernel(taps, dact_f, dact_r, own_ref, mate_ref, other_ref, flat, keep_ref, send_ref, line, grad):
    rows, full = dact_f.shape
    half = keep_ref.shape[1]
    span = own_ref.shape[1]
    seq, chan = lax.axis_index("seq"), lax.axis_index("chan")
    bases = line_of(own_ref, mate_ref, other_ref, line)
    stem_w = flat[...].astype(jnp.bfloat16)
    result = jnp.zeros(grad.shape, jnp.float32)
    for strand, dact in enumerate((dact_f, dact_r)):
        hot = indicators(bases, taps, span - 2 * (taps // 2), rows, strand == 1)
        if strand == 0:
            inside = dot(hot, centre_rows(taps), ((0,), (0,)))[:, :1]
        stem = dot(hot, stem_w, ((0,), (0,))).astype(jnp.bfloat16).astype(jnp.float32)
        _, tanh_val = gelu_value(stem)
        dstem = 0.5 * dact[...] * gelu_slope(stem, tanh_val) * inside
        high = dstem.astype(jnp.bfloat16)
        low = (dstem - high.astype(jnp.float32)).astype(jnp.bfloat16)
        result += dot(hot, high) + dot(hot, low)
    grad[...] = result
    top = send_ref.shape[0]
    keep_ref[:top, :] = own_half(grad, slice(0, top), half, chan)
    send_ref[...] = own_half(grad, slice(0, top), half, 1 - chan)
    per_row = half // span
    shape = (keep_ref.shape[0] - top, half)
    place = lax.broadcasted_iota(jnp.int32, shape, 0) * per_row + lax.broadcasted_iota(jnp.int32, shape, 1) // span
    table = jnp.zeros(shape, jnp.float32)
    for ref, block in ((own_ref, seq), (mate_ref, seq ^ 1)):
        row = jnp.broadcast_to(jnp.concatenate([ref[...].astype(jnp.float32)] * per_row, axis=1), shape)
        table = jnp.where(place == block, row, table)
    keep_ref[top:, :] = table


def stem_part(dacts, own, mate, other, flat, taps, half):
    full = flat.shape[1]
    span = own.shape[1]
    blocks = lax.axis_size("seq")
    per_row = half // span
    top = round_up(4 * taps, 8)
    rows = top + round_up((blocks + per_row - 1) // per_row, 8)
    return pl.pallas_call(
        functools.partial(stem_kernel, taps),
        out_shape=tuple(jax.ShapeDtypeStruct((r, half), jnp.float32) for r in (rows, top)),
        in_specs=[VMEM] * 6,
        out_specs=(VMEM, VMEM),
        scratch_shapes=[pltpu.VMEM((1, 3 * span), jnp.int32), pltpu.VMEM((32, full), jnp.float32)],
        compiler_params=pltpu.CompilerParams(vmem_limit_bytes=LIMIT),
        cost_estimate=CHEAP,
        name="stem_part",
    )(*dacts, own, mate, other, flat)


def blend_kernel(own_ref, mate_ref, other_ref, flat, conv_w, blended_ref, line, act_f, act_r, stem_own):
    taps = conv_w.shape[0]
    span, half = blended_ref.shape
    rows = act_f.shape[0]
    reach = taps // 2
    chan = lax.axis_index("chan")
    bases = line_of(own_ref, mate_ref, other_ref, line)
    stem_w = flat[...].astype(jnp.bfloat16)
    for strand, act in enumerate((act_f, act_r)):
        hot = indicators(bases, taps, span - 2 * reach, rows, strand == 1)
        if strand == 0:
            inside = dot(hot, centre_rows(taps), ((0,), (0,)))[:, :1]
        stem = dot(hot, stem_w, ((0,), (0,))).astype(jnp.bfloat16).astype(jnp.float32)
        value, _ = gelu_value(stem)
        act[...] = (value * inside).astype(jnp.bfloat16).astype(jnp.float32)
        if strand == 0:
            stem_own[...] = stem
        else:
            stem_own[...] += stem
    total = own_half(stem_own, pl.ds(reach, span), half, chan)
    for k in range(taps):
        back = taps - 1 - k
        both = (act_f[k : k + span] + act_r[back : back + span]).astype(jnp.bfloat16)
        total += dot(both, conv_w[k])
    blended_ref[...] = (0.5 * total).astype(jnp.bfloat16)


def blend_part(own, mate, other, flat, conv_w):
    taps, full, half = conv_w.shape
    span = own.shape[1]
    rows = round_up(span + taps - 1, 16)
    return pl.pallas_call(
        blend_kernel,
        out_shape=jax.ShapeDtypeStruct((span, half), jnp.bfloat16),
        in_specs=[VMEM] * 5,
        out_specs=VMEM,
        scratch_shapes=[pltpu.VMEM((1, 3 * span), jnp.int32)] + [pltpu.VMEM((rows, full), jnp.float32) for _ in range(3)],
        compiler_params=pltpu.CompilerParams(vmem_limit_bytes=LIMIT),
        cost_estimate=pl.CostEstimate(flops=2 * 10**9, bytes_accessed=0, transcendentals=0),
        name="blend_part",
    )(own, mate, other, flat, conv_w)


def grad_kernel(taps, kept, chans, masks, flat, table, *refs):
    blocks, out_ref, line, acts, cots = refs[: len(masks)], *refs[len(masks) :]
    count = sum(map(len, masks))
    span = cots.shape[0] // count
    per_row = table.shape[1] // span
    seq = lax.axis_index("seq")
    line[...] = jnp.full(line.shape, -1, jnp.int32)
    for b in range(count):
        row, lane = b // per_row, b % per_row * span
        line[:, LANES + b * span : LANES + (b + 1) * span] = table[row : row + 1, lane : lane + span].astype(jnp.int32)
    for ref, own in zip(blocks, masks):
        for i, mask in enumerate(own):
            cots[pl.ds(pl.multiple_of((seq ^ mask) * span, LANES), span), :] = ref[i * span : (i + 1) * span, :]
    bases = line[...]
    width = bases.shape[1]
    full = flat.shape[1]
    own_w = pltpu.roll(flat[...], lax.rem(full - seq * (full // count), full), 1)[:, :chans].astype(jnp.bfloat16)
    values = []
    reach = taps // 2
    for reverse in (False, True):
        hot = indicators(bases, taps, -reach, width, reverse)
        stem = dot(own_w, hot, ((0,), (0,))).astype(jnp.bfloat16).astype(jnp.float32)
        value, _ = gelu_value(stem)
        values.append(jnp.where(bases >= 0, value, 0.0).astype(jnp.bfloat16).astype(jnp.float32))
    for k in range(taps):
        move = (reach - k) % width
        back = (k - reach) % width
        ahead = pltpu.roll(values[0], move, 1) if move else values[0]
        behind = pltpu.roll(values[1], back, 1) if back else values[1]
        acts[k * chans : (k + 1) * chans, :] = (ahead + behind)[:, LANES : LANES + count * span].astype(jnp.bfloat16)
    total = 0.5 * dot(acts[...], cots[...])
    for k in range(taps):
        out_ref[k] = total[k * chans : k * chans + kept]


def grad_part(flat, table, arrays, masks, span, taps):
    full = flat.shape[1]
    half = arrays[0].shape[1]
    count = sum(map(len, masks))
    kept = full // count
    chans = round_up(kept, 16)
    return pl.pallas_call(
        functools.partial(grad_kernel, taps, kept, chans, masks),
        out_shape=jax.ShapeDtypeStruct((taps, kept, half), jnp.float32),
        in_specs=[VMEM] * (2 + len(arrays)),
        out_specs=VMEM,
        scratch_shapes=[
            pltpu.VMEM((1, count * span + 2 * LANES), jnp.int32),
            pltpu.VMEM((taps * chans, count * span), jnp.bfloat16),
            pltpu.VMEM((count * span, half), jnp.bfloat16),
        ],
        compiler_params=pltpu.CompilerParams(vmem_limit_bytes=LIMIT),
        cost_estimate=pl.CostEstimate(flops=25 * 10**8, bytes_accessed=0, transcendentals=0),
        name="grad_part",
    )(flat, table, *arrays)


def after(value, *others):
    return lax.optimization_barrier((value, *others))[0]


def on_device(tokens, stem_weight, conv_weight, cotangent):
    count = lax.axis_size("seq")
    span = tokens.shape[0]
    taps, full, half = conv_weight.shape
    far = range(count - 4, 0, -4)

    bases = tokens.reshape(1, span)
    far_cot = [swap(cotangent, m) for m in far]
    other = swap_next_chip(bases)
    mate = swap(after(bases, other), 1)
    flat = flat_part(after(stem_weight, other))
    dacts = back_part(after(cotangent, flat), conv_weight)
    keep, send = stem_part(dacts, bases, mate, other, flat, taps, half)
    got = swap_chan(send)
    top = got.shape[0]
    total = jnp.concatenate([keep[:top] + got, keep[top:]])
    total = total + swap(total, 2)
    here = jnp.concatenate([cotangent, *far_cot])
    there = swap(here, 2)
    here_mate = swap(here, 1)
    blended = blend_part(bases, mate, other, flat, conv_weight)
    for bit in range(2, (count - 1).bit_length()):
        total = total + swap(total, 1 << bit)
    total, here_mate, there, blended = lax.optimization_barrier((total, here_mate, there, blended))
    there_mate = swap(there, 1)
    total, table = total[:top], total[top:]
    masks = [0, *far]
    masks = [[m + i for m in masks] for i in range(4)]
    grad_conv = grad_part(flat, table, [here, here_mate, there, there_mate], masks, span, taps)
    total = after(total, grad_conv) + swap(total, 1)
    return blended, grad_conv, total[: 4 * taps].reshape(taps, 4, half)


def solution(mesh):
    return jax.shard_map(
        on_device,
        mesh=mesh,
        in_specs=(P("seq"), P(), P(None, None, "chan"), P("seq", "chan")),
        out_specs=(P("seq", "chan"), P(None, "seq", "chan"), P(None, None, "chan")),
        check_vma=False,
    )
```

```python
import functools
import math

import jax
import jax.numpy as jnp
from jax import lax
from jax.experimental import pallas as pl
from jax.experimental.pallas import tpu as pltpu
from jax.sharding import PartitionSpec as P

VMEM = pl.BlockSpec(memory_space=pltpu.VMEM)
LANES = 128
LIMIT = 24 * 2**20
CHEAP = pl.CostEstimate(flops=0, bytes_accessed=0, transcendentals=0)


def swap(value, mask):
    count = lax.axis_size("seq")
    return lax.ppermute(value, "seq", [(i, i ^ mask) for i in range(count)])


def swap_chan(value):
    count = lax.axis_size("chan")
    return lax.ppermute(value, "chan", [(i, i ^ 1) for i in range(count)])


def swap_next_chip(value):
    count = lax.axis_size("seq")
    pairs = [(i, i + 1) for i in range(1, count - 1, 2)]
    return lax.ppermute(value, "seq", pairs + [(b, a) for a, b in pairs])


def round_up(value, step):
    return (value + step - 1) // step * step


def gelu_value(stem):
    tanh_val = jnp.tanh(math.sqrt(2.0 / math.pi) * (stem + 0.044715 * stem * stem * stem))
    return 0.5 * stem * (1.0 + tanh_val), tanh_val


def gelu_slope(stem, tanh_val):
    coeff = math.sqrt(2.0 / math.pi)
    return 0.5 * (1.0 + tanh_val) + 0.5 * stem * (1.0 - tanh_val * tanh_val) * coeff * (
        1.0 + 3.0 * 0.044715 * stem * stem
    )


def indicators(bases, taps, shift, width, reverse):
    rows = 32
    size = bases.shape[1]
    wide = jnp.broadcast_to(bases, (rows, size))
    row = lax.broadcasted_iota(jnp.int32, (rows, width), 0)
    if reverse:
        row = 4 * taps - 1 - row
    seen = jnp.full((rows, width), -1, jnp.int32)
    for k in range(taps):
        move = (-shift - k) % size
        moved = (pltpu.roll(wide, move, 1) if move else wide)[:, :width]
        seen = jnp.where((row >= 4 * k) & (row < 4 * k + 4), moved, seen)
    return (seen == (row & 3)).astype(jnp.float32).astype(jnp.bfloat16)


def dot(left, right, dims=((1,), (0,))):
    return lax.dot_general(left, right, (dims, ((), ())), preferred_element_type=jnp.float32)


def mark_kernel(out_ref):
    out_ref[...] = jnp.zeros_like(out_ref)


def mark_part():
    return pl.pallas_call(
        mark_kernel,
        out_shape=jax.ShapeDtypeStruct((8, LANES), jnp.float32),
        out_specs=VMEM,
        cost_estimate=pl.CostEstimate(flops=6 * 10**9, bytes_accessed=0, transcendentals=0),
        name="mark_part",
    )()


def line_of(own_ref, mate_ref, other_ref, line):
    span = own_ref.shape[1]
    seq = lax.axis_index("seq")
    even = lax.rem(seq, 2) == 0
    mate, other = mate_ref[...], other_ref[...]
    line[:, :span] = jnp.where(even, other, mate)
    line[:, span : 2 * span] = own_ref[...]
    line[:, 2 * span :] = jnp.where(even, mate, other)
    at = lax.broadcasted_iota(jnp.int32, line.shape, 1) + (seq - 1) * span
    return jnp.where((at >= 0) & (at < span * lax.axis_size("seq")), line[...], -1)


def centre_rows(taps):
    row = lax.broadcasted_iota(jnp.int32, (32, LANES), 0)
    reach = taps // 2
    return ((row >= 4 * reach) & (row < 4 * reach + 4)).astype(jnp.float32).astype(jnp.bfloat16)


def own_half(ref, rows, half, chan):
    return ref[rows, pl.ds(pl.multiple_of(chan * half, LANES), half)]


def back_kernel(cot_ref, conv_w, stem_w_ref, dact_f, dact_r, flat_ref):
    taps = conv_w.shape[0]
    flat_ref[...] = jnp.zeros_like(flat_ref)
    for k in range(taps):
        flat_ref[4 * k : 4 * k + 4, :] = stem_w_ref[k].astype(jnp.float32)
    span = cot_ref.shape[0]
    dact_f[...] = jnp.zeros_like(dact_f)
    dact_r[...] = jnp.zeros_like(dact_r)
    cot = cot_ref[...]
    for k in range(taps):
        part = dot(cot, conv_w[k], ((1,), (1,)))
        dact_f[k : k + span] += part
        dact_r[taps - 1 - k : taps - 1 - k + span] += part


def back_part(cot, conv_w, stem_w):
    taps, full, _ = conv_w.shape
    rows = round_up(cot.shape[0] + taps - 1, 16)
    return pl.pallas_call(
        back_kernel,
        out_shape=tuple(jax.ShapeDtypeStruct((r, full), jnp.float32) for r in (rows, rows, 32)),
        in_specs=[VMEM] * 3,
        out_specs=(VMEM, VMEM, VMEM),
        compiler_params=pltpu.CompilerParams(vmem_limit_bytes=LIMIT),
        cost_estimate=pl.CostEstimate(flops=14 * 10**8, bytes_accessed=0, transcendentals=0),
        name="back_part",
    )(cot, conv_w, stem_w)


def stem_kernel(taps, dact_f, dact_r, own_ref, mate_ref, other_ref, flat, keep_ref, send_ref, line, grad):
    rows, full = dact_f.shape
    half = keep_ref.shape[1]
    span = own_ref.shape[1]
    seq, chan = lax.axis_index("seq"), lax.axis_index("chan")
    bases = line_of(own_ref, mate_ref, other_ref, line)
    stem_w = flat[...].astype(jnp.bfloat16)
    result = jnp.zeros(grad.shape, jnp.float32)
    for strand, dact in enumerate((dact_f, dact_r)):
        hot = indicators(bases, taps, span - 2 * (taps // 2), rows, strand == 1)
        if strand == 0:
            inside = dot(hot, centre_rows(taps), ((0,), (0,)))[:, :1]
        stem = dot(hot, stem_w, ((0,), (0,))).astype(jnp.bfloat16).astype(jnp.float32)
        _, tanh_val = gelu_value(stem)
        dstem = 0.5 * dact[...] * gelu_slope(stem, tanh_val) * inside
        high = dstem.astype(jnp.bfloat16)
        low = (dstem - high.astype(jnp.float32)).astype(jnp.bfloat16)
        result += dot(hot, high) + dot(hot, low)
    grad[...] = result
    top = send_ref.shape[0]
    keep_ref[:top, :] = own_half(grad, slice(0, top), half, chan)
    send_ref[...] = own_half(grad, slice(0, top), half, 1 - chan)
    per_row = half // span
    shape = (keep_ref.shape[0] - top, half)
    place = lax.broadcasted_iota(jnp.int32, shape, 0) * per_row + lax.broadcasted_iota(jnp.int32, shape, 1) // span
    table = jnp.zeros(shape, jnp.float32)
    for ref, block in ((own_ref, seq), (mate_ref, seq ^ 1)):
        row = jnp.broadcast_to(jnp.concatenate([ref[...].astype(jnp.float32)] * per_row, axis=1), shape)
        table = jnp.where(place == block, row, table)
    keep_ref[top:, :] = table


def stem_part(dacts, own, mate, other, flat, taps, half):
    full = flat.shape[1]
    span = own.shape[1]
    blocks = lax.axis_size("seq")
    per_row = half // span
    top = round_up(4 * taps, 8)
    rows = top + round_up((blocks + per_row - 1) // per_row, 8)
    return pl.pallas_call(
        functools.partial(stem_kernel, taps),
        out_shape=tuple(jax.ShapeDtypeStruct((r, half), jnp.float32) for r in (rows, top)),
        in_specs=[VMEM] * 6,
        out_specs=(VMEM, VMEM),
        scratch_shapes=[pltpu.VMEM((1, 3 * span), jnp.int32), pltpu.VMEM((32, full), jnp.float32)],
        compiler_params=pltpu.CompilerParams(vmem_limit_bytes=LIMIT),
        cost_estimate=CHEAP,
        name="stem_part",
    )(*dacts, own, mate, other, flat)


def blend_kernel(mark_ref, own_ref, mate_ref, other_ref, flat, conv_w, blended_ref, line, act_f, act_r, stem_own):
    taps = conv_w.shape[0]
    span, half = blended_ref.shape
    rows = act_f.shape[0]
    reach = taps // 2
    chan = lax.axis_index("chan")
    bases = line_of(own_ref, mate_ref, other_ref, line)
    stem_w = flat[...].astype(jnp.bfloat16)
    for strand, act in enumerate((act_f, act_r)):
        hot = indicators(bases, taps, span - 2 * reach, rows, strand == 1)
        if strand == 0:
            inside = dot(hot, centre_rows(taps), ((0,), (0,)))[:, :1]
        stem = dot(hot, stem_w, ((0,), (0,))).astype(jnp.bfloat16).astype(jnp.float32)
        value, _ = gelu_value(stem)
        act[...] = (value * inside).astype(jnp.bfloat16).astype(jnp.float32)
        if strand == 0:
            stem_own[...] = stem
        else:
            stem_own[...] += stem
    total = own_half(stem_own, pl.ds(reach, span), half, chan)
    for k in range(taps):
        back = taps - 1 - k
        both = (act_f[k : k + span] + act_r[back : back + span]).astype(jnp.bfloat16)
        total += dot(both, conv_w[k])
    blended_ref[...] = (0.5 * total).astype(jnp.bfloat16)


def blend_part(mark, own, mate, other, flat, conv_w):
    taps, full, half = conv_w.shape
    span = own.shape[1]
    rows = round_up(span + taps - 1, 16)
    return pl.pallas_call(
        blend_kernel,
        out_shape=jax.ShapeDtypeStruct((span, half), jnp.bfloat16),
        in_specs=[pl.BlockSpec(memory_space=pl.ANY)] + [VMEM] * 5,
        out_specs=VMEM,
        scratch_shapes=[pltpu.VMEM((1, 3 * span), jnp.int32)] + [pltpu.VMEM((rows, full), jnp.float32) for _ in range(3)],
        compiler_params=pltpu.CompilerParams(vmem_limit_bytes=LIMIT),
        cost_estimate=pl.CostEstimate(flops=2 * 10**9, bytes_accessed=0, transcendentals=0),
        name="blend_part",
    )(mark, own, mate, other, flat, conv_w)


def pair_dots(acts_ref, own_ref, mate_ref, masks, cots):
    span = own_ref.shape[0] // len(masks)
    seq = lax.axis_index("seq")
    total = jnp.zeros((acts_ref.shape[0], own_ref.shape[1]), jnp.float32)
    for i, mask in enumerate(masks):
        block = seq ^ mask
        rows = slice(i * span, (i + 1) * span)
        for ref, side in ((own_ref, block & 1), (mate_ref, 1 - (block & 1))):
            cots[pl.ds(pl.multiple_of((2 * i + side) * span, LANES), span), :] = ref[rows, :]
        at = pl.multiple_of((block >> 1) * (2 * span), 2 * LANES)
        total += dot(acts_ref[:, pl.ds(at, 2 * span)], cots[2 * i * span : 2 * (i + 1) * span, :])
    return total


def acts_kernel(taps, chans, masks, flat, table, here_ref, mate_ref, acts_ref, total_ref, line, cots):
    span = here_ref.shape[0] // len(masks)
    count = 4 * len(masks)
    per_row = table.shape[1] // span
    seq = lax.axis_index("seq")
    line[...] = jnp.full(line.shape, -1, jnp.int32)
    for b in range(count):
        row, lane = b // per_row, b % per_row * span
        line[:, LANES + b * span : LANES + (b + 1) * span] = table[row : row + 1, lane : lane + span].astype(jnp.int32)
    bases = line[...]
    width = bases.shape[1]
    full = flat.shape[1]
    own_w = pltpu.roll(flat[...], lax.rem(full - seq * (full // count), full), 1)[:, :chans].astype(jnp.bfloat16)
    values = []
    reach = taps // 2
    for reverse in (False, True):
        hot = indicators(bases, taps, -reach, width, reverse)
        stem = dot(own_w, hot, ((0,), (0,))).astype(jnp.bfloat16).astype(jnp.float32)
        value, _ = gelu_value(stem)
        values.append(jnp.where(bases >= 0, value, 0.0).astype(jnp.bfloat16).astype(jnp.float32))
    for k in range(taps):
        move = (reach - k) % width
        back = (k - reach) % width
        ahead = pltpu.roll(values[0], move, 1) if move else values[0]
        behind = pltpu.roll(values[1], back, 1) if back else values[1]
        acts_ref[k * chans : (k + 1) * chans, :] = (ahead + behind)[:, LANES : LANES + count * span].astype(jnp.bfloat16)
    total_ref[...] = pair_dots(acts_ref, here_ref, mate_ref, masks, cots)


def acts_part(flat, table, here, mate, masks, span, taps):
    full, half = flat.shape[1], here.shape[1]
    count = 4 * len(masks)
    chans = round_up(full // count, 16)
    return pl.pallas_call(
        functools.partial(acts_kernel, taps, chans, masks),
        out_shape=(
            jax.ShapeDtypeStruct((taps * chans, count * span), jnp.bfloat16),
            jax.ShapeDtypeStruct((taps * chans, half), jnp.float32),
        ),
        in_specs=[VMEM] * 4,
        out_specs=(VMEM, VMEM),
        scratch_shapes=[
            pltpu.VMEM((1, count * span + 2 * LANES), jnp.int32),
            pltpu.VMEM((2 * here.shape[0], half), jnp.bfloat16),
        ],
        compiler_params=pltpu.CompilerParams(vmem_limit_bytes=LIMIT),
        cost_estimate=pl.CostEstimate(flops=2 * 10**9, bytes_accessed=0, transcendentals=0),
        name="acts_part",
    )(flat, table, here, mate)


def grad_kernel(masks, acts_ref, there_ref, mate_ref, first_ref, stem_ref, got_ref, out_ref, stem_out, cots):
    taps, kept, _ = out_ref.shape
    stem = stem_ref[...] + got_ref[...]
    for k in range(taps):
        stem_out[k] = stem[4 * k : 4 * k + 4]
    chans = acts_ref.shape[0] // taps
    total = 0.5 * (first_ref[...] + pair_dots(acts_ref, there_ref, mate_ref, masks, cots))
    for k in range(taps):
        out_ref[k] = total[k * chans : k * chans + kept]


def grad_part(acts, there, mate, first, stem, got, masks, taps, kept):
    half = there.shape[1]
    return pl.pallas_call(
        functools.partial(grad_kernel, masks),
        out_shape=(
            jax.ShapeDtypeStruct((taps, kept, half), jnp.float32),
            jax.ShapeDtypeStruct((taps, 4, half), jnp.float32),
        ),
        in_specs=[VMEM] * 6,
        out_specs=(VMEM, VMEM),
        scratch_shapes=[pltpu.VMEM((2 * there.shape[0], half), jnp.bfloat16)],
        compiler_params=pltpu.CompilerParams(vmem_limit_bytes=LIMIT),
        cost_estimate=pl.CostEstimate(flops=10**9, bytes_accessed=0, transcendentals=0),
        name="grad_part",
    )(acts, there, mate, first, stem, got)


def after(value, *others):
    return lax.optimization_barrier((value, *others))[0]


def on_device(tokens, stem_weight, conv_weight, cotangent):
    count = lax.axis_size("seq")
    span = tokens.shape[0]
    taps, full, half = conv_weight.shape
    far = range(count - 4, 0, -4)

    mark = mark_part()
    bases = after(tokens.reshape(1, span), mark)
    other = swap_next_chip(bases)
    far_cot = [swap(cotangent, m) for m in far]
    mate = swap(after(bases, other), 1)
    *dacts, flat = back_part(after(cotangent, other), conv_weight, stem_weight)
    keep, send = stem_part(dacts, bases, mate, other, flat, taps, half)
    got = swap_chan(send)
    top = got.shape[0]
    total = jnp.concatenate([keep[:top] + got, keep[top:]])
    total = total + swap(total, 2)
    here = jnp.concatenate([cotangent, *far_cot])
    there = swap(here, 2)
    here_mate = swap(here, 1)
    blended = blend_part(mark, bases, mate, other, flat, conv_weight)
    for bit in range(2, (count - 1).bit_length()):
        total = total + swap(total, 1 << bit)
    total, here_mate, there, blended = lax.optimization_barrier((total, here_mate, there, blended))
    there_mate = swap(there, 1)
    total, table = total[:top], total[top:]
    masks = [0, *far]
    acts, first = acts_part(flat, table, here, here_mate, masks, span, taps)
    grad_conv, grad_stem = grad_part(
        acts, there, there_mate, first, total, swap(total, 1), [m + 2 for m in masks], taps, full // count
    )
    return blended, grad_conv, grad_stem


def solution(mesh):
    return jax.shard_map(
        on_device,
        mesh=mesh,
        in_specs=(P("seq"), P(), P(None, None, "chan"), P("seq", "chan")),
        out_specs=(P("seq", "chan"), P(None, "seq", "chan"), P(None, None, "chan")),
        check_vma=False,
    )
```

```python
import functools
import math

import jax
import jax.numpy as jnp
from jax import lax
from jax.experimental import pallas as pl
from jax.experimental.pallas import tpu as pltpu
from jax.sharding import PartitionSpec as P

VMEM = pl.BlockSpec(memory_space=pltpu.VMEM)
LANES = 128
LIMIT = 24 * 2**20
CHEAP = pl.CostEstimate(flops=0, bytes_accessed=0, transcendentals=0)


def swap(value, mask):
    count = lax.axis_size("seq")
    return lax.ppermute(value, "seq", [(i, i ^ mask) for i in range(count)])


def swap_chan(value):
    count = lax.axis_size("chan")
    return lax.ppermute(value, "chan", [(i, i ^ 1) for i in range(count)])


def swap_next_chip(value):
    count = lax.axis_size("seq")
    pairs = [(i, i + 1) for i in range(1, count - 1, 2)]
    return lax.ppermute(value, "seq", pairs + [(b, a) for a, b in pairs])


def round_up(value, step):
    return (value + step - 1) // step * step


def gelu_parts(stem):
    square = stem * stem
    coeff = math.sqrt(2.0 / math.pi)
    return 0.5 + 0.5 * jnp.tanh(stem * (coeff + coeff * 0.044715 * square)), square


def gelu_slope(stem, step, square):
    coeff = math.sqrt(2.0 / math.pi)
    return step + step * (1.0 - step) * stem * (2.0 * coeff + 2.0 * coeff * 3.0 * 0.044715 * square)


def indicators(bases, taps, shift, width):
    size = bases.shape[1]
    wide = jnp.broadcast_to(bases, (8, size))
    moved = []
    for k in range(taps):
        move = (-shift - k) % size
        moved.append((pltpu.roll(wide, move, 1) if move else wide)[:, :width])
    none = jnp.full((8, width), -1, jnp.int32)
    row = lax.broadcasted_iota(jnp.int32, (8, width), 0)
    results = []
    for order, letter in ((moved, row & 3), (moved[::-1], 3 - (row & 3))):
        order = order + [none] * (8 - taps)
        groups = [jnp.where(row < 4, order[2 * g], order[2 * g + 1]) == letter for g in range(4)]
        results.append(jnp.concatenate([g.astype(jnp.float32) for g in groups]).astype(jnp.bfloat16))
    return results


def dot(left, right, dims=((1,), (0,))):
    return lax.dot_general(left, right, (dims, ((), ())), preferred_element_type=jnp.float32)


def mark_kernel(out_ref):
    out_ref[...] = jnp.zeros_like(out_ref)


def mark_part():
    return pl.pallas_call(
        mark_kernel,
        out_shape=jax.ShapeDtypeStruct((8, LANES), jnp.float32),
        out_specs=VMEM,
        cost_estimate=pl.CostEstimate(flops=6 * 10**9, bytes_accessed=0, transcendentals=0),
        name="mark_part",
    )()


def line_of(own_ref, mate_ref, other_ref, line):
    span = own_ref.shape[1]
    seq = lax.axis_index("seq")
    even = lax.rem(seq, 2) == 0
    mate, other = mate_ref[...], other_ref[...]
    line[:, :span] = jnp.where(even, other, mate)
    line[:, span : 2 * span] = own_ref[...]
    line[:, 2 * span :] = jnp.where(even, mate, other)
    at = lax.broadcasted_iota(jnp.int32, line.shape, 1) + (seq - 1) * span
    return jnp.where((at >= 0) & (at < span * lax.axis_size("seq")), line[...], -1)


def centre_rows(taps):
    row = lax.broadcasted_iota(jnp.int32, (32, LANES), 0)
    reach = taps // 2
    return ((row >= 4 * reach) & (row < 4 * reach + 4)).astype(jnp.float32).astype(jnp.bfloat16)


def own_half(ref, rows, half, chan):
    return ref[rows, pl.ds(pl.multiple_of(chan * half, LANES), half)]


def back_kernel(cot_ref, conv_w, stem_w_ref, dact_f, dact_r, flat_ref):
    taps = conv_w.shape[0]
    flat_ref[...] = jnp.zeros_like(flat_ref)
    for k in range(taps):
        flat_ref[4 * k : 4 * k + 4, :] = stem_w_ref[k].astype(jnp.float32)
    span = cot_ref.shape[0]
    dact_f[...] = jnp.zeros_like(dact_f)
    dact_r[...] = jnp.zeros_like(dact_r)
    cot = cot_ref[...]
    for k in range(taps):
        part = dot(cot, conv_w[k], ((1,), (1,)))
        dact_f[k : k + span] += part
        dact_r[taps - 1 - k : taps - 1 - k + span] += part


def back_part(cot, conv_w, stem_w):
    taps, full, _ = conv_w.shape
    rows = round_up(cot.shape[0] + taps - 1, 16)
    return pl.pallas_call(
        back_kernel,
        out_shape=tuple(jax.ShapeDtypeStruct((r, full), jnp.float32) for r in (rows, rows, 32)),
        in_specs=[VMEM] * 3,
        out_specs=(VMEM, VMEM, VMEM),
        compiler_params=pltpu.CompilerParams(vmem_limit_bytes=LIMIT),
        cost_estimate=pl.CostEstimate(flops=14 * 10**8, bytes_accessed=0, transcendentals=0),
        name="back_part",
    )(cot, conv_w, stem_w)


def stem_kernel(taps, dact_f, dact_r, own_ref, mate_ref, other_ref, flat, keep_ref, send_ref, line, grad):
    rows, full = dact_f.shape
    half = full // lax.axis_size("chan")
    span = own_ref.shape[1]
    seq, chan = lax.axis_index("seq"), lax.axis_index("chan")
    bases = line_of(own_ref, mate_ref, other_ref, line)
    stem_w = flat[...].astype(jnp.bfloat16)
    result = jnp.zeros(grad.shape, jnp.float32)
    hots = indicators(bases, taps, span - 2 * (taps // 2), rows)
    for strand, (dact, hot) in enumerate(zip((dact_f, dact_r), hots)):
        if strand == 0:
            inside = dot(hot, centre_rows(taps), ((0,), (0,)))[:, :1]
        stem = dot(hot, stem_w, ((0,), (0,))).astype(jnp.bfloat16).astype(jnp.float32)
        step, square = gelu_parts(stem)
        dstem = dact[...] * gelu_slope(stem, step, square) * (0.5 * inside)
        high = dstem.astype(jnp.bfloat16)
        low = (dstem - high.astype(jnp.float32)).astype(jnp.bfloat16)
        result += dot(hot, high) + dot(hot, low)
    grad[...] = result
    count = 4 * taps
    top = send_ref.shape[0]
    send_ref[...] = jnp.zeros_like(send_ref)
    keep_ref[:top, :] = jnp.zeros((top, LANES), jnp.float32)
    for j in range(half // LANES):
        rows = slice(j * count, (j + 1) * count)
        for ref, side in ((keep_ref, chan), (send_ref, 1 - chan)):
            ref[rows, :] = grad[:count, pl.ds(pl.multiple_of(side * half + j * LANES, LANES), LANES)]
    lines = span // LANES
    place = lax.broadcasted_iota(jnp.int32, (keep_ref.shape[0] - top, LANES), 0)
    table = jnp.zeros(place.shape, jnp.float32)
    for ref, block in ((own_ref, seq), (mate_ref, seq ^ 1)):
        for i in range(lines):
            row = jnp.broadcast_to(ref[:, i * LANES : (i + 1) * LANES].astype(jnp.float32), place.shape)
            table = jnp.where(place == block * lines + i, row, table)
    keep_ref[top:, :] = table


def stem_part(dacts, own, mate, other, flat, taps, half):
    full = flat.shape[1]
    span = own.shape[1]
    blocks = lax.axis_size("seq")
    top = round_up(4 * taps * (half // LANES), 8)
    rows = top + round_up(blocks * span // LANES, 8)
    return pl.pallas_call(
        functools.partial(stem_kernel, taps),
        out_shape=tuple(jax.ShapeDtypeStruct((r, LANES), jnp.float32) for r in (rows, top)),
        in_specs=[VMEM] * 6,
        out_specs=(VMEM, VMEM),
        scratch_shapes=[pltpu.VMEM((1, 3 * span), jnp.int32), pltpu.VMEM((32, full), jnp.float32)],
        compiler_params=pltpu.CompilerParams(vmem_limit_bytes=LIMIT),
        cost_estimate=CHEAP,
        name="stem_part",
    )(*dacts, own, mate, other, flat)


def blend_kernel(mark_ref, own_ref, mate_ref, other_ref, flat, conv_w, blended_ref, line, act_f, act_r, stem_own):
    taps = conv_w.shape[0]
    span, half = blended_ref.shape
    rows = act_f.shape[0]
    reach = taps // 2
    chan = lax.axis_index("chan")
    bases = line_of(own_ref, mate_ref, other_ref, line)
    stem_w = flat[...].astype(jnp.bfloat16)
    hots = indicators(bases, taps, span - 2 * reach, rows)
    for strand, (act, hot) in enumerate(zip((act_f, act_r), hots)):
        if strand == 0:
            inside = dot(hot, centre_rows(taps), ((0,), (0,)))[:, :1]
        stem = dot(hot, stem_w, ((0,), (0,))).astype(jnp.bfloat16).astype(jnp.float32)
        step, _ = gelu_parts(stem)
        act[...] = (stem * step * inside).astype(jnp.bfloat16).astype(jnp.float32)
        if strand == 0:
            stem_own[...] = stem
        else:
            stem_own[...] += stem
    total = own_half(stem_own, pl.ds(reach, span), half, chan)
    for k in range(taps):
        back = taps - 1 - k
        both = (act_f[k : k + span] + act_r[back : back + span]).astype(jnp.bfloat16)
        total += dot(both, conv_w[k])
    blended_ref[...] = (0.5 * total).astype(jnp.bfloat16)


def blend_part(mark, own, mate, other, flat, conv_w):
    taps, full, half = conv_w.shape
    span = own.shape[1]
    rows = round_up(span + taps - 1, 16)
    return pl.pallas_call(
        blend_kernel,
        out_shape=jax.ShapeDtypeStruct((span, half), jnp.bfloat16),
        in_specs=[pl.BlockSpec(memory_space=pl.ANY)] + [VMEM] * 5,
        out_specs=VMEM,
        scratch_shapes=[pltpu.VMEM((1, 3 * span), jnp.int32)] + [pltpu.VMEM((rows, full), jnp.float32) for _ in range(3)],
        compiler_params=pltpu.CompilerParams(vmem_limit_bytes=LIMIT),
        cost_estimate=pl.CostEstimate(flops=2 * 10**9, bytes_accessed=0, transcendentals=0),
        name="blend_part",
    )(mark, own, mate, other, flat, conv_w)


def pair_dots(acts_ref, own_ref, mate_ref, masks, cots):
    span = own_ref.shape[0] // len(masks)
    seq = lax.axis_index("seq")
    total = jnp.zeros((acts_ref.shape[0], own_ref.shape[1]), jnp.float32)
    for i, mask in enumerate(masks):
        block = seq ^ mask
        rows = slice(i * span, (i + 1) * span)
        for ref, side in ((own_ref, block & 1), (mate_ref, 1 - (block & 1))):
            cots[pl.ds(pl.multiple_of((2 * i + side) * span, LANES), span), :] = ref[rows, :]
        at = pl.multiple_of((block >> 1) * (2 * span), 2 * LANES)
        total += dot(acts_ref[:, pl.ds(at, 2 * span)], cots[2 * i * span : 2 * (i + 1) * span, :])
    return total


def acts_kernel(taps, chans, masks, flat, table, here_ref, mate_ref, acts_ref, total_ref, line, cots):
    span = here_ref.shape[0] // len(masks)
    count = 4 * len(masks)
    lines = span // LANES
    seq = lax.axis_index("seq")
    line[...] = jnp.full(line.shape, -1, jnp.int32)
    for b in range(count):
        for i in range(lines):
            at = LANES + b * span + i * LANES
            line[:, at : at + LANES] = table[b * lines + i : b * lines + i + 1, :].astype(jnp.int32)
    bases = line[...]
    width = bases.shape[1]
    full = flat.shape[1]
    own_w = pltpu.roll(flat[...], lax.rem(full - seq * (full // count), full), 1)[:, :chans].astype(jnp.bfloat16)
    values = []
    reach = taps // 2
    for hot in indicators(bases, taps, -reach, width):
        stem = dot(own_w, hot, ((0,), (0,))).astype(jnp.bfloat16).astype(jnp.float32)
        step, _ = gelu_parts(stem)
        values.append(jnp.where(bases >= 0, stem * step, 0.0).astype(jnp.bfloat16))
    for k in range(taps):
        move = (reach - k) % width
        back = (k - reach) % width
        ahead = pltpu.roll(values[0], move, 1) if move else values[0]
        behind = pltpu.roll(values[1], back, 1) if back else values[1]
        acts_ref[k * chans : (k + 1) * chans, :] = (ahead + behind)[:, LANES : LANES + count * span]
    total_ref[...] = pair_dots(acts_ref, here_ref, mate_ref, masks, cots)


def acts_part(flat, table, here, mate, masks, span, taps):
    full, half = flat.shape[1], here.shape[1]
    count = 4 * len(masks)
    chans = round_up(full // count, 16)
    return pl.pallas_call(
        functools.partial(acts_kernel, taps, chans, masks),
        out_shape=(
            jax.ShapeDtypeStruct((taps * chans, count * span), jnp.bfloat16),
            jax.ShapeDtypeStruct((taps * chans, half), jnp.float32),
        ),
        in_specs=[VMEM] * 4,
        out_specs=(VMEM, VMEM),
        scratch_shapes=[
            pltpu.VMEM((1, count * span + 2 * LANES), jnp.int32),
            pltpu.VMEM((2 * here.shape[0], half), jnp.bfloat16),
        ],
        compiler_params=pltpu.CompilerParams(vmem_limit_bytes=LIMIT),
        cost_estimate=pl.CostEstimate(flops=2 * 10**9, bytes_accessed=0, transcendentals=0),
        name="acts_part",
    )(flat, table, here, mate)


def grad_kernel(masks, acts_ref, there_ref, mate_ref, first_ref, stem_ref, got_ref, out_ref, stem_out, cots):
    taps, kept, _ = out_ref.shape
    stem = stem_ref[...] + got_ref[...]
    for k in range(taps):
        for j in range(stem_out.shape[2] // LANES):
            at = 4 * (j * taps + k)
            stem_out[k, :, j * LANES : (j + 1) * LANES] = stem[at : at + 4]
    chans = acts_ref.shape[0] // taps
    total = 0.5 * (first_ref[...] + pair_dots(acts_ref, there_ref, mate_ref, masks, cots))
    for k in range(taps):
        out_ref[k] = total[k * chans : k * chans + kept]


def grad_part(acts, there, mate, first, stem, got, masks, taps, kept):
    half = there.shape[1]
    return pl.pallas_call(
        functools.partial(grad_kernel, masks),
        out_shape=(
            jax.ShapeDtypeStruct((taps, kept, half), jnp.float32),
            jax.ShapeDtypeStruct((taps, 4, half), jnp.float32),
        ),
        in_specs=[VMEM] * 6,
        out_specs=(VMEM, VMEM),
        scratch_shapes=[pltpu.VMEM((2 * there.shape[0], half), jnp.bfloat16)],
        compiler_params=pltpu.CompilerParams(vmem_limit_bytes=LIMIT),
        cost_estimate=pl.CostEstimate(flops=10**9, bytes_accessed=0, transcendentals=0),
        name="grad_part",
    )(acts, there, mate, first, stem, got)


def after(value, *others):
    return lax.optimization_barrier((value, *others))[0]


def on_device(tokens, stem_weight, conv_weight, cotangent):
    count = lax.axis_size("seq")
    span = tokens.shape[0]
    taps, full, half = conv_weight.shape
    far = range(count - 4, 0, -4)

    mark = mark_part()
    bases = after(tokens.reshape(1, span), mark)
    other = swap_next_chip(bases)
    far_cot = [swap(cotangent, m) for m in far]
    mate = swap(after(bases, other), 1)
    *dacts, flat = back_part(after(cotangent, other), conv_weight, stem_weight)
    keep, send = stem_part(dacts, bases, mate, other, flat, taps, half)
    got = swap_chan(send)
    top = got.shape[0]
    total = jnp.concatenate([keep[:top] + got, keep[top:]])
    total = total + swap(total, 2)
    here = jnp.concatenate([cotangent, *far_cot])
    there = swap(here, 2)
    here_mate = swap(here, 1)
    blended = blend_part(mark, bases, mate, other, flat, conv_weight)
    for bit in range(2, (count - 1).bit_length()):
        total = total + swap(total, 1 << bit)
    total, here_mate, there, blended = lax.optimization_barrier((total, here_mate, there, blended))
    there_mate = swap(there, 1)
    total, table = total[:top], total[top:]
    masks = [0, *far]
    acts, first = acts_part(flat, table, here, here_mate, masks, span, taps)
    grad_conv, grad_stem = grad_part(
        acts, there, there_mate, first, total, swap(total, 1), [m + 2 for m in masks], taps, full // count
    )
    return blended, grad_conv, grad_stem


def solution(mesh):
    return jax.shard_map(
        on_device,
        mesh=mesh,
        in_specs=(P("seq"), P(), P(None, None, "chan"), P("seq", "chan")),
        out_specs=(P("seq", "chan"), P(None, "seq", "chan"), P(None, None, "chan")),
        check_vma=False,
    )
```

```python
import functools
import math

import jax
import jax.numpy as jnp
from jax import lax
from jax.experimental import pallas as pl
from jax.experimental.pallas import tpu as pltpu
from jax.sharding import PartitionSpec as P

VMEM = pl.BlockSpec(memory_space=pltpu.VMEM)
LANES = 128
LIMIT = 24 * 2**20
CHEAP = pl.CostEstimate(flops=0, bytes_accessed=0, transcendentals=0)


def swap(value, mask):
    count = lax.axis_size("seq")
    return lax.ppermute(value, "seq", [(i, i ^ mask) for i in range(count)])


def swap_chan(value):
    count = lax.axis_size("chan")
    return lax.ppermute(value, "chan", [(i, i ^ 1) for i in range(count)])


def swap_next_chip(value):
    count = lax.axis_size("seq")
    pairs = [(i, i + 1) for i in range(1, count - 1, 2)]
    return lax.ppermute(value, "seq", pairs + [(b, a) for a, b in pairs])


def round_up(value, step):
    return (value + step - 1) // step * step


def gelu_parts(stem):
    square = stem * stem
    coeff = math.sqrt(2.0 / math.pi)
    return 0.5 + 0.5 * jnp.tanh(stem * (coeff + coeff * 0.044715 * square)), square


def gelu_slope(stem, step, square):
    coeff = math.sqrt(2.0 / math.pi)
    return step + step * (1.0 - step) * stem * (2.0 * coeff + 2.0 * coeff * 3.0 * 0.044715 * square)


def indicators(bases, taps, shift, width):
    size = bases.shape[1]
    wide = jnp.broadcast_to(bases, (8, size))
    moved = []
    for k in range(taps):
        move = (-shift - k) % size
        moved.append((pltpu.roll(wide, move, 1) if move else wide)[:, :width])
    none = jnp.full((8, width), -1, jnp.int32)
    row = lax.broadcasted_iota(jnp.int32, (8, width), 0)
    results = []
    for order, letter in ((moved, row & 3), (moved[::-1], 3 - (row & 3))):
        order = order + [none] * (8 - taps)
        groups = [jnp.where(row < 4, order[2 * g], order[2 * g + 1]) == letter for g in range(4)]
        results.append(jnp.concatenate([g.astype(jnp.float32) for g in groups]).astype(jnp.bfloat16))
    return results


def dot(left, right, dims=((1,), (0,))):
    return lax.dot_general(left, right, (dims, ((), ())), preferred_element_type=jnp.float32)


def mark_kernel(out_ref):
    del out_ref


def mark_part():
    return pl.pallas_call(
        mark_kernel,
        out_shape=jax.ShapeDtypeStruct((8, LANES), jnp.float32),
        out_specs=pl.BlockSpec(memory_space=pl.ANY),
        cost_estimate=pl.CostEstimate(flops=6 * 10**9, bytes_accessed=0, transcendentals=0),
        name="mark_part",
    )()


def line_of(own_ref, mate_ref, other_ref, line):
    span = own_ref.shape[1]
    seq = lax.axis_index("seq")
    even = lax.rem(seq, 2) == 0
    mate, other = mate_ref[...], other_ref[...]
    line[:, :span] = jnp.where(even, other, mate)
    line[:, span : 2 * span] = own_ref[...]
    line[:, 2 * span :] = jnp.where(even, mate, other)
    at = lax.broadcasted_iota(jnp.int32, line.shape, 1) + (seq - 1) * span
    return jnp.where((at >= 0) & (at < span * lax.axis_size("seq")), line[...], -1)


def centre_rows(taps):
    row = lax.broadcasted_iota(jnp.int32, (32, LANES), 0)
    reach = taps // 2
    return ((row >= 4 * reach) & (row < 4 * reach + 4)).astype(jnp.float32).astype(jnp.bfloat16)


def own_half(ref, rows, half, chan):
    return ref[rows, pl.ds(pl.multiple_of(chan * half, LANES), half)]


def back_kernel(cot_ref, conv_w, stem_w_ref, dact_f, dact_r, flat_ref):
    taps = conv_w.shape[0]
    flat_ref[...] = jnp.zeros_like(flat_ref)
    for k in range(taps):
        flat_ref[4 * k : 4 * k + 4, :] = stem_w_ref[k].astype(jnp.float32)
    span = cot_ref.shape[0]
    dact_f[...] = jnp.zeros_like(dact_f)
    dact_r[...] = jnp.zeros_like(dact_r)
    cot = cot_ref[...]
    for k in range(taps):
        part = dot(cot, conv_w[k], ((1,), (1,)))
        dact_f[k : k + span] += part
        dact_r[taps - 1 - k : taps - 1 - k + span] += part


def back_part(cot, conv_w, stem_w):
    taps, full, _ = conv_w.shape
    rows = round_up(cot.shape[0] + taps - 1, 16)
    return pl.pallas_call(
        back_kernel,
        out_shape=tuple(jax.ShapeDtypeStruct((r, full), jnp.float32) for r in (rows, rows, 32)),
        in_specs=[VMEM] * 3,
        out_specs=(VMEM, VMEM, VMEM),
        compiler_params=pltpu.CompilerParams(vmem_limit_bytes=LIMIT),
        cost_estimate=pl.CostEstimate(flops=14 * 10**8, bytes_accessed=0, transcendentals=0),
        name="back_part",
    )(cot, conv_w, stem_w)


def stem_kernel(taps, dact_f, dact_r, own_ref, mate_ref, other_ref, flat, keep_ref, send_ref, line, grad):
    rows, full = dact_f.shape
    half = full // lax.axis_size("chan")
    span = own_ref.shape[1]
    seq, chan = lax.axis_index("seq"), lax.axis_index("chan")
    bases = line_of(own_ref, mate_ref, other_ref, line)
    stem_w = flat[...].astype(jnp.bfloat16)
    result = jnp.zeros(grad.shape, jnp.float32)
    hots = indicators(bases, taps, span - 2 * (taps // 2), rows)
    for strand, (dact, hot) in enumerate(zip((dact_f, dact_r), hots)):
        if strand == 0:
            inside = dot(hot, centre_rows(taps), ((0,), (0,)))[:, :1]
        stem = dot(hot, stem_w, ((0,), (0,))).astype(jnp.bfloat16).astype(jnp.float32)
        step, square = gelu_parts(stem)
        dstem = dact[...] * gelu_slope(stem, step, square) * (0.5 * inside)
        high = dstem.astype(jnp.bfloat16)
        low = (dstem - high.astype(jnp.float32)).astype(jnp.bfloat16)
        result += dot(hot, high) + dot(hot, low)
    grad[...] = result
    count = 4 * taps
    top = send_ref.shape[0]
    send_ref[...] = jnp.zeros_like(send_ref)
    keep_ref[:top, :] = jnp.zeros((top, LANES), jnp.float32)
    for j in range(half // LANES):
        rows = slice(j * count, (j + 1) * count)
        for ref, side in ((keep_ref, chan), (send_ref, 1 - chan)):
            ref[rows, :] = grad[:count, pl.ds(pl.multiple_of(side * half + j * LANES, LANES), LANES)]
    lines = span // LANES
    place = lax.broadcasted_iota(jnp.int32, (keep_ref.shape[0] - top, LANES), 0)
    table = jnp.zeros(place.shape, jnp.float32)
    for ref, block in ((own_ref, seq), (mate_ref, seq ^ 1)):
        for i in range(lines):
            row = jnp.broadcast_to(ref[:, i * LANES : (i + 1) * LANES].astype(jnp.float32), place.shape)
            table = jnp.where(place == block * lines + i, row, table)
    keep_ref[top:, :] = table


def stem_part(dacts, own, mate, other, flat, taps, half):
    full = flat.shape[1]
    span = own.shape[1]
    blocks = lax.axis_size("seq")
    top = round_up(4 * taps * (half // LANES), 8)
    rows = top + round_up(blocks * span // LANES, 8)
    return pl.pallas_call(
        functools.partial(stem_kernel, taps),
        out_shape=tuple(jax.ShapeDtypeStruct((r, LANES), jnp.float32) for r in (rows, top)),
        in_specs=[VMEM] * 6,
        out_specs=(VMEM, VMEM),
        scratch_shapes=[pltpu.VMEM((1, 3 * span), jnp.int32), pltpu.VMEM((32, full), jnp.float32)],
        compiler_params=pltpu.CompilerParams(vmem_limit_bytes=LIMIT),
        cost_estimate=CHEAP,
        name="stem_part",
    )(*dacts, own, mate, other, flat)


def blend_kernel(mark_ref, own_ref, mate_ref, other_ref, flat, conv_w, blended_ref, line, act_f, act_r, stem_own):
    taps = conv_w.shape[0]
    span, half = blended_ref.shape
    rows = act_f.shape[0]
    reach = taps // 2
    chan = lax.axis_index("chan")
    bases = line_of(own_ref, mate_ref, other_ref, line)
    stem_w = flat[...].astype(jnp.bfloat16)
    hots = indicators(bases, taps, span - 2 * reach, rows)
    for strand, (act, hot) in enumerate(zip((act_f, act_r), hots)):
        if strand == 0:
            inside = dot(hot, centre_rows(taps), ((0,), (0,)))[:, :1]
        stem = dot(hot, stem_w, ((0,), (0,))).astype(jnp.bfloat16).astype(jnp.float32)
        step, _ = gelu_parts(stem)
        act[...] = (stem * step * inside).astype(jnp.bfloat16).astype(jnp.float32)
        if strand == 0:
            stem_own[...] = stem
        else:
            stem_own[...] += stem
    total = own_half(stem_own, pl.ds(reach, span), half, chan)
    for k in range(taps):
        back = taps - 1 - k
        both = (act_f[k : k + span] + act_r[back : back + span]).astype(jnp.bfloat16)
        total += dot(both, conv_w[k])
    blended_ref[...] = (0.5 * total).astype(jnp.bfloat16)


def blend_part(mark, own, mate, other, flat, conv_w):
    taps, full, half = conv_w.shape
    span = own.shape[1]
    rows = round_up(span + taps - 1, 16)
    return pl.pallas_call(
        blend_kernel,
        out_shape=jax.ShapeDtypeStruct((span, half), jnp.bfloat16),
        in_specs=[pl.BlockSpec(memory_space=pl.ANY)] + [VMEM] * 5,
        out_specs=VMEM,
        scratch_shapes=[pltpu.VMEM((1, 3 * span), jnp.int32)] + [pltpu.VMEM((rows, full), jnp.float32) for _ in range(3)],
        compiler_params=pltpu.CompilerParams(vmem_limit_bytes=LIMIT),
        cost_estimate=pl.CostEstimate(flops=2 * 10**9, bytes_accessed=0, transcendentals=0),
        name="blend_part",
    )(mark, own, mate, other, flat, conv_w)


def pair_dots(acts_ref, own_ref, mate_ref, masks, cots):
    span = own_ref.shape[0] // len(masks)
    seq = lax.axis_index("seq")
    total = jnp.zeros((acts_ref.shape[0], own_ref.shape[1]), jnp.float32)
    for i, mask in enumerate(masks):
        block = seq ^ mask
        rows = slice(i * span, (i + 1) * span)
        for ref, side in ((own_ref, block & 1), (mate_ref, 1 - (block & 1))):
            cots[pl.ds(pl.multiple_of((2 * i + side) * span, LANES), span), :] = ref[rows, :]
        at = pl.multiple_of((block >> 1) * (2 * span), 2 * LANES)
        total += dot(acts_ref[:, pl.ds(at, 2 * span)], cots[2 * i * span : 2 * (i + 1) * span, :])
    return total


def acts_kernel(taps, chans, masks, flat, table, here_ref, mate_ref, acts_ref, total_ref, line, cots):
    span = here_ref.shape[0] // len(masks)
    count = 4 * len(masks)
    lines = span // LANES
    seq = lax.axis_index("seq")
    line[...] = jnp.full(line.shape, -1, jnp.int32)
    for b in range(count):
        for i in range(lines):
            at = LANES + b * span + i * LANES
            line[:, at : at + LANES] = table[b * lines + i : b * lines + i + 1, :].astype(jnp.int32)
    bases = line[...]
    width = bases.shape[1]
    full = flat.shape[1]
    own_w = pltpu.roll(flat[...], lax.rem(full - seq * (full // count), full), 1)[:, :chans].astype(jnp.bfloat16)
    values = []
    reach = taps // 2
    for hot in indicators(bases, taps, -reach, width):
        stem = dot(own_w, hot, ((0,), (0,))).astype(jnp.bfloat16).astype(jnp.float32)
        step, _ = gelu_parts(stem)
        values.append(jnp.where(bases >= 0, stem * step, 0.0).astype(jnp.bfloat16))
    for k in range(taps):
        move = (reach - k) % width
        back = (k - reach) % width
        ahead = pltpu.roll(values[0], move, 1) if move else values[0]
        behind = pltpu.roll(values[1], back, 1) if back else values[1]
        acts_ref[k * chans : (k + 1) * chans, :] = (ahead + behind)[:, LANES : LANES + count * span]
    total_ref[...] = pair_dots(acts_ref, here_ref, mate_ref, masks, cots)


def acts_part(flat, table, here, mate, masks, span, taps):
    full, half = flat.shape[1], here.shape[1]
    count = 4 * len(masks)
    chans = round_up(full // count, 16)
    return pl.pallas_call(
        functools.partial(acts_kernel, taps, chans, masks),
        out_shape=(
            jax.ShapeDtypeStruct((taps * chans, count * span), jnp.bfloat16),
            jax.ShapeDtypeStruct((taps * chans, half), jnp.float32),
        ),
        in_specs=[VMEM] * 4,
        out_specs=(VMEM, VMEM),
        scratch_shapes=[
            pltpu.VMEM((1, count * span + 2 * LANES), jnp.int32),
            pltpu.VMEM((2 * here.shape[0], half), jnp.bfloat16),
        ],
        compiler_params=pltpu.CompilerParams(vmem_limit_bytes=LIMIT),
        cost_estimate=pl.CostEstimate(flops=2 * 10**9, bytes_accessed=0, transcendentals=0),
        name="acts_part",
    )(flat, table, here, mate)


def grad_kernel(masks, acts_ref, there_ref, mate_ref, first_ref, stem_ref, got_ref, out_ref, stem_out, cots):
    taps, kept, _ = out_ref.shape
    stem = stem_ref[...] + got_ref[...]
    for k in range(taps):
        for j in range(stem_out.shape[2] // LANES):
            at = 4 * (j * taps + k)
            stem_out[k, :, j * LANES : (j + 1) * LANES] = stem[at : at + 4]
    chans = acts_ref.shape[0] // taps
    total = 0.5 * (first_ref[...] + pair_dots(acts_ref, there_ref, mate_ref, masks, cots))
    for k in range(taps):
        out_ref[k] = total[k * chans : k * chans + kept]


def grad_part(acts, there, mate, first, stem, got, masks, taps, kept):
    half = there.shape[1]
    return pl.pallas_call(
        functools.partial(grad_kernel, masks),
        out_shape=(
            jax.ShapeDtypeStruct((taps, kept, half), jnp.float32),
            jax.ShapeDtypeStruct((taps, 4, half), jnp.float32),
        ),
        in_specs=[VMEM] * 6,
        out_specs=(VMEM, VMEM),
        scratch_shapes=[pltpu.VMEM((2 * there.shape[0], half), jnp.bfloat16)],
        compiler_params=pltpu.CompilerParams(vmem_limit_bytes=LIMIT),
        cost_estimate=pl.CostEstimate(flops=10**9, bytes_accessed=0, transcendentals=0),
        name="grad_part",
    )(acts, there, mate, first, stem, got)


def after(value, *others):
    return lax.optimization_barrier((value, *others))[0]


def on_device(tokens, stem_weight, conv_weight, cotangent):
    count = lax.axis_size("seq")
    span = tokens.shape[0]
    taps, full, half = conv_weight.shape
    far = range(count - 4, 0, -4)

    mark = mark_part()
    bases = tokens.reshape(1, span)
    other = swap_next_chip(bases)
    far_cot = [swap(after(cotangent, mark), m) for m in far]
    mate = swap(after(bases, other), 1)
    *dacts, flat = back_part(after(cotangent, other), conv_weight, stem_weight)
    keep, send = stem_part(dacts, bases, mate, other, flat, taps, half)
    got = swap_chan(send)
    top = got.shape[0]
    total = jnp.concatenate([keep[:top] + got, keep[top:]])
    total = total + swap(total, 2)
    here = jnp.concatenate([cotangent, *far_cot])
    there = swap(here, 2)
    here_mate = swap(here, 1)
    blended = blend_part(mark, bases, mate, other, flat, conv_weight)
    for bit in range(2, (count - 1).bit_length()):
        total = total + swap(total, 1 << bit)
    total, here_mate, there, blended = lax.optimization_barrier((total, here_mate, there, blended))
    there_mate = swap(there, 1)
    total, table = total[:top], total[top:]
    masks = [0, *far]
    acts, first = acts_part(flat, table, here, here_mate, masks, span, taps)
    grad_conv, grad_stem = grad_part(
        acts, there, there_mate, first, total, swap(total, 1), [m + 2 for m in masks], taps, full // count
    )
    return blended, grad_conv, grad_stem


def solution(mesh):
    return jax.shard_map(
        on_device,
        mesh=mesh,
        in_specs=(P("seq"), P(), P(None, None, "chan"), P("seq", "chan")),
        out_specs=(P("seq", "chan"), P(None, "seq", "chan"), P(None, None, "chan")),
        check_vma=False,
    )
```
